256 devices in a mesh: gx: 16 (over z, x_lo), gy: 8 (over y, core), gz: 2 (over x_hi).
Axes of the slice: x: 4 (x_hi: 2, x_lo: 2; x = x_hi * 2 + x_lo), y: 4, z: 8, core: 2. Of those that a mesh axis runs over, the one named last changes fastest.
Arguments:
- z_factor: float32 [512, 8, 128, 128], P(('gx', 'gy', 'gz')), may hold values from -0.16 to 1.16
- z_columns: int32 [512, 8], replicated, may hold values from 0 to 511, as said below
- p_columns: int32 [512, 8], replicated, may hold values from 0 to 511, as said below
- d_density: float32 [512, 8, 128, 128], P(('gx', 'gy', 'gz')), may hold values from -6 to 6
Outputs:
- adjoint_x: float32 [512, 8, 128, 128], P(('gx', 'gy', 'gz'))
- adjoint_f: float32 [512, 8, 128, 128], P(('gx', 'gy', 'gz'))
The draws below stay inside these ranges and needn't reach their ends.
Inputs may be any that keep to these rules, and one draw needn't show every extreme that they name: `z_columns`: block row i belongs to atom box i // 2; box b has coordinates (b // 16, (b // 2) % 8, b % 2). Entry [i, 0] is i; the other entries of row i are distinct block rows of the same box or of the boxes next to it by one step along one coordinate, periodically. Exactly one of them lies in i's own box, and at most 2 in any one other box. `p_columns`: same form and same bounds as z_columns.
All inputs are finite; a program needn't handle non-finite values.
Results may differ from the reference program's by a relative error of at most 0.0003.
Values sent between devices are 32-bit elements; how exact they have to be, the bound alone decides.
A program may use at most 128 MiB of HBM per device.

```python
import jax
import jax.numpy as jnp
from jax import lax

BLOCK = 128
SLOTS = 8
ROWS_DEV = 2
BLOCK_ROWS = 512
N_GX = 16
N_GY = 8
N_GZ = 2


def offsets_all_drawn():
    found = [(0, 0, 0)]
    for axis, count in ((0, N_GX), (1, N_GY), (2, N_GZ)):
        moves = [1, -1] if count > 2 else [1] if count == 2 else []
        for move in moves:
            found.append(tuple((move if place == axis else 0 for place in range(3))))
    return found


def near_rows_drawn(row):
    box = row // ROWS_DEV
    coord_z = box % N_GZ
    coord_y = box // N_GZ % N_GY
    coord_x = box // (N_GZ * N_GY)
    pieces = []
    for off_x, off_y, off_z in offsets_all_drawn():
        linear = ((coord_x + off_x) % N_GX * N_GY + (coord_y + off_y) % N_GY) * N_GZ + (coord_z + off_z) % N_GZ
        pieces.append((linear * ROWS_DEV)[..., None] + jnp.arange(ROWS_DEV, dtype=jnp.int32))
    return jnp.concatenate(pieces, axis=-1).astype(jnp.int32)


def pattern(key):
    rows = jnp.arange(BLOCK_ROWS, dtype=jnp.int32)
    cand = near_rows_drawn(rows)
    width = cand.shape[1]
    boxes = width // ROWS_DEV
    own_count = min(ROWS_DEV - 1, 2)
    rest_count = SLOTS - 3 - own_count
    bits = jax.random.randint(jax.random.fold_in(key, 1), cand.shape, 0, 1 << 20, dtype=jnp.int32)
    score = bits * width + jnp.arange(width, dtype=jnp.int32)[None, :]
    score = jnp.where(cand == rows[:, None], jnp.int32(-1), score)
    grouped = score.reshape((BLOCK_ROWS, boxes, ROWS_DEV))
    cand_grouped = cand.reshape((BLOCK_ROWS, boxes, ROWS_DEV))
    order = jnp.argsort(-grouped, axis=2).astype(jnp.int32)
    top_two = jnp.take_along_axis(cand_grouped, order[:, :, :2], axis=2)
    own_part = top_two[:, 0, :own_count]
    full_box = jax.random.randint(jax.random.fold_in(key, 2), (BLOCK_ROWS,), 1, boxes, dtype=jnp.int32)
    full_part = jnp.take_along_axis(top_two, full_box[:, None, None], axis=1)[:, 0, :]
    pool = top_two[:, 1:, :].reshape((BLOCK_ROWS, 2 * (boxes - 1)))
    pool_box = jnp.repeat(jnp.arange(1, boxes, dtype=jnp.int32), 2)
    bits_pool = jax.random.randint(jax.random.fold_in(key, 3), pool.shape, 0, 1 << 20, dtype=jnp.int32)
    score_pool = bits_pool * pool.shape[1] + jnp.arange(pool.shape[1], dtype=jnp.int32)[None, :]
    score_pool = jnp.where(pool_box[None, :] == full_box[:, None], jnp.int32(-1), score_pool)
    order_pool = jnp.argsort(-score_pool, axis=1).astype(jnp.int32)
    rest_part = jnp.take_along_axis(pool, order_pool[:, :rest_count], axis=1)
    return jnp.concatenate([rows[:, None], own_part, full_part, rest_part], axis=1).astype(jnp.int32)


def draw_z_columns(key, part):
    return pattern(jax.random.fold_in(key, 11))


def draw_p_columns(key, part):
    return pattern(jax.random.fold_in(key, 23))


def draw_z_factor(key, part):
    shape = (BLOCK_ROWS, SLOTS, BLOCK, BLOCK)
    noise = jnp.clip(jax.random.normal(key, shape, jnp.float32), -4.0, 4.0)
    first = (jnp.arange(SLOTS) == 0).astype(jnp.float32)
    return 0.04 * noise + first[None, :, None, None] * jnp.eye(BLOCK, dtype=jnp.float32)[None, None]


def shard_levels(key, shape, cuts, low, top_value):
    def one(position, blocks):
        heights = jax.random.uniform(jax.random.fold_in(jax.random.fold_in(key, 6), position), (blocks,), jnp.float32, low / len(cuts), top_value / len(cuts))
        return jnp.repeat(jnp.exp(heights), shape[position] // blocks).reshape((-1,) + (1,) * (len(shape) - position - 1))

    level = one(*cuts[0])
    for cut in cuts[1:]:
        level = level * one(*cut)
    return level


def scatter_about(own_key, shape, scale, limit, cuts=(), held_as=jnp.bfloat16):
    entries = jax.random.normal(own_key, shape, jnp.float32) * scale
    if len(cuts) > 0:
        entries = shard_levels(own_key, shape, cuts, -0.22, 0.18) * entries
    return jnp.clip(entries, min=-limit, max=limit).astype(held_as)


def setup_inputs(seed: int = 0) -> dict:
    splits = jax.random.split(jax.random.key(seed), 5)
    return {
        "z_factor": draw_z_factor(jax.random.fold_in(splits[4], 71), 0),
        "z_columns": draw_z_columns(jax.random.fold_in(splits[4], 71), 0),
        "p_columns": draw_p_columns(jax.random.fold_in(splits[4], 71), 0),
        "d_density": scatter_about(splits[3], (BLOCK_ROWS, SLOTS, BLOCK, BLOCK), 1.0, 6.0, ((0, 256),), jnp.float32),
    }


HIGH = lax.Precision.HIGHEST


def offsets_all():
    found = [(0, 0, 0)]
    for axis, count in ((0, N_GX), (1, N_GY), (2, N_GZ)):
        moves = [1, -1] if count > 2 else ([1] if count == 2 else [])
        for move in moves:
            found.append(tuple(move if place == axis else 0 for place in range(3)))
    return found


def near_rows(row):
    box = row // ROWS_DEV
    coord_z = box % N_GZ
    coord_y = (box // N_GZ) % N_GY
    coord_x = box // (N_GZ * N_GY)
    pieces = []
    for off_x, off_y, off_z in offsets_all():
        linear = (((coord_x + off_x) % N_GX) * N_GY + (coord_y + off_y) % N_GY) * N_GZ + (coord_z + off_z) % N_GZ
        pieces.append((linear * ROWS_DEV)[..., None] + jnp.arange(ROWS_DEV, dtype=jnp.int32))
    return jnp.concatenate(pieces, axis=-1).astype(jnp.int32)


def pick(blocks, keys, targets):
    equal = targets[..., None] == keys
    found = jnp.any(equal, axis=-1)
    where = jnp.argmax(equal, axis=-1).astype(jnp.int32)
    taken = jnp.take(blocks, where, axis=0)
    return jnp.where(found[..., None, None], taken, jnp.zeros((), blocks.dtype))


def reference(z_factor, z_columns, p_columns, d_density):
    own = jnp.arange(BLOCK_ROWS, dtype=jnp.int32)
    z_keys = (own[:, None] * BLOCK_ROWS + z_columns).astype(jnp.int32)
    p_keys = (own[:, None] * BLOCK_ROWS + p_columns).astype(jnp.int32)

    def near(table, keys, row):
        cand = near_rows(row)
        return table[cand].reshape((-1, BLOCK, BLOCK)), keys[cand].reshape(-1), cand

    def step_y(row):
        blocks, keys, cand = near(z_factor, z_keys, row)
        cols = p_columns[row]
        chosen = pick(blocks, keys, cols[None, :] * BLOCK_ROWS + cols[:, None])
        return jnp.einsum("tab,stbc->sac", d_density[row], chosen, precision=HIGH)

    y_prod = lax.map(step_y, own)

    def step_x(row):
        zblocks, zkeys, cand = near(z_factor, z_keys, row)
        yblocks, ykeys, cand = near(y_prod, p_keys, row)
        z_side = pick(zblocks, zkeys, cand * BLOCK_ROWS + row)
        y_side = pick(yblocks, ykeys, cand[None, :] * BLOCK_ROWS + p_columns[row][:, None])
        return jnp.einsum("cba,scbd->sad", z_side, y_side, precision=HIGH)

    adjoint_x = lax.map(step_x, own)

    def step_w(row):
        xblocks, xkeys, cand = near(adjoint_x, p_keys, row)
        chosen = pick(xblocks, xkeys, z_columns[row][None, :] * BLOCK_ROWS + p_columns[row][:, None])
        return jnp.einsum("uab,subc->sac", z_factor[row], chosen, precision=HIGH)

    w_prod = lax.map(step_w, own)

    def step_f(row):
        zblocks, zkeys, cand = near(z_factor, z_keys, row)
        cols = p_columns[row]
        chosen = pick(zblocks, zkeys, cols[:, None] * BLOCK_ROWS + cols[None, :])
        return jnp.einsum("tab,stcb->sac", w_prod[row], chosen, precision=HIGH)

    adjoint_f = lax.map(step_f, own)
    return adjoint_x, adjoint_f
```

```python
import jax
import jax.numpy as jnp
from jax import lax
from jax.experimental import pallas as pl
from jax.experimental.pallas import tpu as pltpu
from jax.sharding import PartitionSpec as P

MESH = pl.DeviceIdType.MESH
BLK = 128
WIDE = 256
SLOTS = 8
GX, GY, GZ = 16, 8, 2
ROWS = 512
OWN = 5
NN = (((1,), (0,)), ((), ()))
TN = (((0,), (0,)), ((), ()))
NT = (((1,), (1,)), ((), ()))


def split(x):
    hi = x.astype(jnp.bfloat16)
    return hi, (x - hi.astype(jnp.float32)).astype(jnp.bfloat16)


def product(a, b, dims):
    a_hi, a_lo = split(a)
    b_hi, b_lo = split(b)

    def dot(x, y):
        return lax.dot_general(x, y, dims, preferred_element_type=jnp.float32)

    return dot(a_hi, b_hi) + (dot(a_hi, b_lo) + dot(a_lo, b_hi))


def kernel(
    cols, z_hbm, d_hbm, ox_hbm, of_hbm,
    z_in, d_in, ox, of, zd, dd, zr, zx, yd, yr, yx, ad, ar, an, wd, stz, sty,
    z_at, z_has, p_at, p_has, o_at, n_has,
    local_sem, send_sem, recv_sem,
):
    gx, gy, gz = lax.axis_index("gx"), lax.axis_index("gy"), lax.axis_index("gz")
    sx = 1 - 2 * lax.rem(gx, 2)
    sy = 1 - 2 * lax.rem(gy, 2)
    near = (gx + sx, gy, gz)
    far = (lax.rem(gx - sx + GX, GX), gy, gz)
    over = (gx, gy, 1 - gz)
    core = (gx, gy + sy, gz)
    side = (gx, lax.rem(gy - sy + GY, GY), gz)
    to_z = (lax.rem(gx + 2 * sx + GX, GX), gy, gz)
    from_z = (lax.rem(gx - 2 * sx + GX, GX), gy, gz)
    cross = (gx + sx, gy, 1 - gz)

    def box(where):
        return (where[0] * GY + where[1]) * GZ + where[2]

    boxes = [box(w) for w in (near, far, over, core, side, (gx, gy, gz))]

    load_z = pltpu.make_async_copy(z_hbm, z_in, local_sem.at[0])
    load_d = pltpu.make_async_copy(d_hbm, d_in, local_sem.at[1])
    load_z.start()
    load_d.start()

    barrier = pltpu.get_barrier_semaphore()
    for where in (near, core, side, from_z, cross):
        pl.semaphore_signal(barrier, inc=1, device_id=where, device_id_type=MESH)

    def table(base, at, has):
        for r in range(2):
            row = base + (boxes[OWN] * 2 + r) * SLOTS
            found = [cols[row + s] for s in range(SLOTS)]
            for q in (5, 2, 1, 0, 3, 4):
                for c in range(2):
                    target = boxes[q] * 2 + c
                    slot, hit = jnp.int32(0), jnp.int32(0)
                    for s in range(SLOTS):
                        same = found[s] == target
                        slot = jnp.where(same, s, slot)
                        hit = jnp.where(same, 1, hit)
                    at[r * 12 + q * 2 + c] = slot
                    has[r * 12 + q * 2 + c] = hit

    def spread(blocks, at, has, dense, q):
        for r in range(2):
            for c in range(2):
                i = r * 12 + q * 2 + c
                block = blocks[r * SLOTS + at[i]]
                dense[q, r * BLK : (r + 1) * BLK, c * BLK : (c + 1) * BLK] = jnp.where(has[i] > 0, block, 0.0)

    def keep(x, flags):
        halves = [
            jnp.concatenate([jnp.where(flags[2 * r + c] > 0, x[r * BLK : (r + 1) * BLK, c * BLK : (c + 1) * BLK], 0.0) for c in range(2)], axis=1)
            for r in range(2)
        ]
        return jnp.concatenate(halves, axis=0)

    def own_flags(q):
        return [p_has[r * 12 + q * 2 + c] for r in range(2) for c in range(2)]

    def copy(i, src, dst, where):
        return pltpu.make_async_remote_copy(
            src_ref=src, dst_ref=dst, send_sem=send_sem.at[i], recv_sem=recv_sem.at[i], device_id=where, device_id_type=MESH
        )

    table(0, z_at, z_has)
    load_z.wait()
    spread(z_in, z_at, z_has, zd, OWN)
    pl.semaphore_wait(barrier, 5)

    c = [
        copy(0, zd.at[OWN], zr.at[0], near),
        copy(1, zd.at[2], stz.at[1], near),
        copy(2, zd.at[1], stz.at[0], near),
        copy(3, zd.at[0], zx.at[0], near),
        copy(4, yd.at[2], sty.at[1], near),
        copy(5, yd.at[1], sty.at[0], near),
        copy(6, yd.at[0], yx.at[0], near),
        copy(7, yd.at[OWN], yr.at[0], near),
        copy(8, ad.at[OWN], ar.at[0], near),
    ]
    for q, where in ((3, core), (4, side)):
        i = 9 + 5 * (q - 3)
        c += [
            copy(i, zd.at[OWN], zr.at[q], where),
            copy(i + 1, zd.at[q], zx.at[q], where),
            copy(i + 2, yd.at[q], yx.at[q], where),
            copy(i + 3, yd.at[OWN], yr.at[q], where),
            copy(i + 4, ad.at[OWN], ar.at[q], where),
        ]
    for n, (q, where) in enumerate(((1, to_z), (2, cross))):
        i = 19 + 5 * n
        c += [
            copy(i, zr.at[0], zr.at[q], where),
            copy(i + 1, stz.at[n], zx.at[q], where),
            copy(i + 2, sty.at[n], yx.at[q], where),
            copy(i + 3, yr.at[0], yr.at[q], where),
            copy(i + 4, ar.at[0], ar.at[q], where),
        ]
    NEAR, CORE, SIDE, FAR, OVER = 0, 9, 14, 19, 24

    c[CORE].start()
    c[SIDE].start()
    c[0].start()
    for q, i in ((2, 1), (1, 2), (0, 3), (3, CORE + 1), (4, SIDE + 1)):
        spread(z_in, z_at, z_has, zd, q)
        c[i].start()

    table(ROWS * SLOTS, p_at, p_has)
    for r in range(2):
        row = ROWS * SLOTS + (boxes[OWN] * 2 + r) * SLOTS
        for s in range(SLOTS):
            column = cols[row + s]
            place = jnp.int32(0)
            for q in range(6):
                for k in range(2):
                    place = jnp.where(column == boxes[q] * 2 + k, q * 2 + k, place)
            o_at[r * SLOTS + s] = place
    for q in range(5):
        for r in range(2):
            row = ROWS * SLOTS + (boxes[q] * 2 + r) * SLOTS
            found = [cols[row + s] for s in range(SLOTS)]
            for k in range(2):
                hit = jnp.int32(0)
                for s in range(SLOTS):
                    hit = jnp.where(found[s] == boxes[OWN] * 2 + k, 1, hit)
                n_has[q * 4 + r * 2 + k] = hit
    load_d.wait()
    for q in (5, 3, 4, 0, 2, 1):
        spread(d_in, p_at, p_has, dd, q)

    @pl.loop(0, 6)
    def _(q):
        yd[q] = product(dd[OWN], zd[q], NN)

    def finish_y(q):
        yd[q] = keep(yd[q] + product(dd[q], zr[q], NN), own_flags(q))

    def gather_y(q):
        yd[OWN] += product(dd[q], zx[q], NN)

    c[CORE].wait_recv()
    finish_y(3)
    c[CORE + 2].start()
    c[SIDE].wait_recv()
    finish_y(4)
    c[SIDE + 2].start()
    c[0].wait_recv()
    c[FAR].start()
    c[OVER].start()
    finish_y(0)
    c[CORE + 1].wait_recv()
    gather_y(3)
    c[SIDE + 1].wait_recv()
    gather_y(4)
    c[1].wait_recv()
    c[OVER + 1].start()
    c[OVER].wait_recv()
    finish_y(2)
    c[4].start()
    c[FAR].wait_recv()
    finish_y(1)
    c[5].start()
    c[6].start()
    c[2].wait_recv()
    c[FAR + 1].start()
    c[OVER + 1].wait_recv()
    gather_y(2)
    c[3].wait_recv()
    gather_y(0)
    c[FAR + 1].wait_recv()
    gather_y(1)
    c[7].start()
    c[CORE + 3].start()
    c[SIDE + 3].start()

    @pl.loop(0, 6)
    def _(q):
        ad[q] = product(zd[OWN], yd[q], TN)

    def gather_a(q):
        ad[OWN] += product(zx[q], yx[q], TN)

    c[CORE + 2].wait_recv()
    gather_a(3)
    c[SIDE + 2].wait_recv()
    gather_a(4)
    c[4].wait_recv()
    c[OVER + 2].start()
    c[5].wait_recv()
    c[FAR + 2].start()
    c[6].wait_recv()
    gather_a(0)
    c[OVER + 2].wait_recv()
    gather_a(2)
    c[FAR + 2].wait_recv()
    gather_a(1)
    c[8].start()
    c[CORE + 4].start()
    c[SIDE + 4].start()

    c[7].wait_recv()
    c[FAR + 3].start()
    c[OVER + 3].start()

    @pl.loop(0, 5)
    def _(q):
        x = product(zr[q], yx[q], TN) + product(zd[q], yd[OWN], TN)
        an[q] = keep(x, [n_has[q * 4 + k] for k in range(4)])

    wd[OWN] = product(zd[OWN], ad[OWN], NN)

    @pl.loop(0, 5)
    def _(q):
        wd[OWN] += product(zd[q], an[q], NN)

    c[CORE + 3].wait_recv()
    c[SIDE + 3].wait_recv()
    c[FAR + 3].wait_recv()
    c[OVER + 3].wait_recv()

    @pl.loop(0, 5)
    def _(q):
        ad[q] = keep(ad[q] + product(zx[q], yr[q], TN), own_flags(q))
        wd[q] = product(zd[OWN], ad[q], NN)

    def collect(dense, out):
        for r in range(2):
            for s in range(SLOTS):
                place = o_at[r * SLOTS + s]
                both = dense[lax.div(place, 2), r * BLK : (r + 1) * BLK]
                out[r * SLOTS + s] = jnp.where(lax.rem(place, 2) > 0, both[:, BLK:], both[:, :BLK])

    collect(ad, ox)
    store_x = pltpu.make_async_copy(ox, ox_hbm, local_sem.at[2])
    store_x.start()

    c[8].wait_recv()
    c[FAR + 4].start()
    c[OVER + 4].start()
    yf = wd
    c[CORE + 4].wait_recv()
    c[SIDE + 4].wait_recv()
    c[FAR + 4].wait_recv()
    c[OVER + 4].wait_recv()

    an[0] = product(wd[OWN], zd[OWN], NT)

    @pl.loop(0, 5)
    def _(q):
        w = keep(wd[q] + product(zd[q], ar[q], NN), own_flags(q))
        an[0] += product(w, zd[q], NT)
        yf[q] = product(wd[OWN], zx[q], NT) + product(w, zr[q], NT)

    wd[OWN] = an[0]
    collect(wd, of)
    store_f = pltpu.make_async_copy(of, of_hbm, local_sem.at[3])
    store_f.start()
    for one in c:
        one.wait_send()
    store_x.wait()
    store_f.wait()


def shards(z_factor, z_columns, p_columns, d_density):
    cols = jnp.concatenate([z_columns.reshape(-1), p_columns.reshape(-1)])
    tiles = (2 * SLOTS, BLK, BLK)
    wide = (WIDE, WIDE)
    f32 = jnp.float32
    counts = [6, 6, 5, 5, 6, 5, 5, 6, 5, 5, 6, 2, 2]
    out_x, out_f = pl.pallas_call(
        kernel,
        out_shape=[jax.ShapeDtypeStruct(tiles, f32)] * 2,
        in_specs=[pl.BlockSpec(memory_space=pltpu.SMEM)] + [pl.BlockSpec(memory_space=pl.ANY)] * 2,
        out_specs=[pl.BlockSpec(memory_space=pl.ANY)] * 2,
        scratch_shapes=[pltpu.VMEM(tiles, f32)] * 4
        + [pltpu.VMEM((n,) + wide, f32) for n in counts]
        + [pltpu.SMEM((n,), jnp.int32) for n in (24, 24, 24, 24, 16, 20)]
        + [pltpu.SemaphoreType.DMA((4,)), pltpu.SemaphoreType.DMA((29,)), pltpu.SemaphoreType.DMA((29,))],
        compiler_params=pltpu.CompilerParams(collective_id=0, has_side_effects=True, vmem_limit_bytes=48 * 1024 * 1024),
    )(cols, z_factor.reshape(tiles), d_density.reshape(tiles))
    shape = z_factor.shape
    return out_x.reshape(shape), out_f.reshape(shape)


def solution(mesh):
    spec = P(("gx", "gy", "gz"), None, None, None)
    return jax.shard_map(shards, mesh=mesh, in_specs=(spec, P(), P(), spec), out_specs=(spec, spec), check_vma=False)
```

```python
import jax
import jax.numpy as jnp
from jax import lax
from jax.experimental import pallas as pl
from jax.experimental.pallas import tpu as pltpu
from jax.sharding import PartitionSpec as P

MESH = pl.DeviceIdType.MESH
BLK = 128
WIDE = 256
SLOTS = 8
GX, GY, GZ = 16, 8, 2
ROWS = 512
OWN = 5
NN = (((1,), (0,)), ((), ()))
TN = (((0,), (0,)), ((), ()))
NT = (((1,), (1,)), ((), ()))


def split(x):
    hi = x.astype(jnp.bfloat16)
    return hi, (x - hi.astype(jnp.float32)).astype(jnp.bfloat16)


def product(a, b, dims):
    a_hi, a_lo = split(a)
    b_hi, b_lo = split(b)

    def dot(x, y):
        return lax.dot_general(x, y, dims, preferred_element_type=jnp.float32)

    return dot(a_hi, b_hi) + (dot(a_hi, b_lo) + dot(a_lo, b_hi))


def kernel(
    zc_hbm, pc_hbm, z_hbm, d_hbm, ox_hbm, of_hbm,
    z_in, d_in, ox, of, zd, dd, zr, zx, yd, yr, yx, ad, ar, an, wd, fd,
    z_cols, p_cols, z_at, z_has, p_at, p_has, o_at, n_has,
    local_sem, send_sem, recv_sem,
):
    gx, gy, gz = lax.axis_index("gx"), lax.axis_index("gy"), lax.axis_index("gz")
    sx = 1 - 2 * lax.rem(gx, 2)
    sy = 1 - 2 * lax.rem(gy, 2)
    near = (gx + sx, gy, gz)
    far = (lax.rem(gx - sx + GX, GX), gy, gz)
    over = (gx, gy, 1 - gz)
    core = (gx, gy + sy, gz)
    side = (gx, lax.rem(gy - sy + GY, GY), gz)
    to_z = (lax.rem(gx + 2 * sx + GX, GX), gy, gz)
    from_z = (lax.rem(gx - 2 * sx + GX, GX), gy, gz)
    cross = (gx + sx, gy, 1 - gz)

    def box(where):
        return (where[0] * GY + where[1]) * GZ + where[2]

    boxes = [box(w) for w in (near, far, over, core, side, (gx, gy, gz))]

    load_z = pltpu.make_async_copy(z_hbm, z_in, local_sem.at[0])
    load_d = pltpu.make_async_copy(d_hbm, d_in, local_sem.at[1])
    load_zc = pltpu.make_async_copy(zc_hbm, z_cols, local_sem.at[4])
    load_pc = pltpu.make_async_copy(pc_hbm, p_cols, local_sem.at[5])
    load_zc.start()
    load_z.start()
    load_pc.start()
    load_d.start()

    barrier = pltpu.get_barrier_semaphore()
    for where in (near, far, over, core, side, from_z, cross):
        pl.semaphore_signal(barrier, inc=1, device_id=where, device_id_type=MESH)

    def table(cols, at, has):
        for r in range(2):
            row = boxes[OWN] * 2 + r
            found = [cols[s, row] for s in range(SLOTS)]
            for q in (5, 2, 1, 0, 3, 4):
                for c in range(2):
                    target = boxes[q] * 2 + c
                    slot, hit = jnp.int32(0), jnp.int32(0)
                    for s in range(SLOTS):
                        same = found[s] == target
                        slot = jnp.where(same, s, slot)
                        hit = jnp.where(same, 1, hit)
                    at[r * 12 + q * 2 + c] = slot
                    has[r * 12 + q * 2 + c] = hit

    def spread(blocks, at, has, dense, q):
        for r in range(2):
            for c in range(2):
                i = r * 12 + q * 2 + c
                block = blocks[r * SLOTS + at[i]]
                dense[q, r * BLK : (r + 1) * BLK, c * BLK : (c + 1) * BLK] = jnp.where(has[i] > 0, block, 0.0)

    def keep(x, flags):
        halves = [
            jnp.concatenate([jnp.where(flags[2 * r + c] > 0, x[r * BLK : (r + 1) * BLK, c * BLK : (c + 1) * BLK], 0.0) for c in range(2)], axis=1)
            for r in range(2)
        ]
        return jnp.concatenate(halves, axis=0)

    def own_flags(q):
        return [p_has[r * 12 + q * 2 + c] for r in range(2) for c in range(2)]

    def copy(i, src, dst, where):
        return pltpu.make_async_remote_copy(
            src_ref=src, dst_ref=dst, send_sem=send_sem.at[i], recv_sem=recv_sem.at[i], device_id=where, device_id_type=MESH
        )

    load_zc.wait()
    table(z_cols, z_at, z_has)
    load_z.wait()
    spread(z_in, z_at, z_has, zd, OWN)
    pl.semaphore_wait(barrier, 7)

    c = {}

    def message(name, src, dst, where):
        c[name] = copy(len(c), src, dst, where)

    half = [pl.ds(0, BLK), pl.ds(BLK, BLK)]
    message("z0", zd.at[OWN], zr.at[0], near)
    for q, where in ((3, core), (4, side)):
        message(f"z{q}", zd.at[OWN], zr.at[q], where)
        message(f"y{q}", yd.at[OWN], yr.at[q], where)
        message(f"a{q}", ad.at[OWN], ar.at[q], where)
    for q, where in enumerate((near, far, over, core, side)):
        message(f"zx{q}", zd.at[q], zx.at[q], where)
        message(f"yx{q}", yd.at[q], yx.at[q], where)
    for h in range(2):
        message(f"y0{h}", yd.at[OWN, half[h]], yr.at[0, half[h]], near)
        message(f"a0{h}", ad.at[OWN, half[h]], ar.at[0, half[h]], near)
    for q, where in ((1, to_z), (2, cross)):
        message(f"z{q}", zr.at[0], zr.at[q], where)
        for h in range(2):
            message(f"y{q}{h}", yr.at[0, half[h]], yr.at[q, half[h]], where)
            message(f"a{q}{h}", ar.at[0, half[h]], ar.at[q, half[h]], where)

    def send(*names):
        for name in names:
            c[name].start()

    def arrive(*names):
        for name in names:
            c[name].wait_recv()

    def tables():
        table(p_cols, p_at, p_has)
        for r in range(2):
            row = boxes[OWN] * 2 + r
            for s in range(SLOTS):
                column = p_cols[s, row]
                place = jnp.int32(0)
                for q in range(6):
                    for k in range(2):
                        place = jnp.where(column == boxes[q] * 2 + k, q * 2 + k, place)
                o_at[r * SLOTS + s] = place
        for q in range(5):
            for r in range(2):
                row = boxes[q] * 2 + r
                found = [p_cols[s, row] for s in range(SLOTS)]
                for k in range(2):
                    hit = jnp.int32(0)
                    for s in range(SLOTS):
                        hit = jnp.where(found[s] == boxes[OWN] * 2 + k, 1, hit)
                    n_has[q * 4 + r * 2 + k] = hit

    send("z0", "z3", "z4")
    for q in (2, 1, 0, 3, 4):
        spread(z_in, z_at, z_has, zd, q)
        send(f"zx{q}")

    load_pc.wait()
    tables()
    load_d.wait()
    for q in (5, 3, 4, 0, 2, 1):
        spread(d_in, p_at, p_has, dd, q)

    @pl.loop(0, 6)
    def _(q):
        yd[q] = product(dd[OWN], zd[q], NN)

    def finish_y(q):
        yd[q] = keep(yd[q] + product(dd[q], zr[q], NN), own_flags(q))

    def gather_y(q):
        yd[OWN] += product(dd[q], zx[q], NN)

    arrive("z3")
    finish_y(3)
    send("yx3")
    arrive("z4")
    finish_y(4)
    send("yx4")
    arrive("z0")
    send("z1", "z2")
    finish_y(0)
    arrive("zx3")
    gather_y(3)
    arrive("zx4")
    gather_y(4)
    arrive("z2")
    finish_y(2)
    send("yx2")
    arrive("z1")
    finish_y(1)
    send("yx1", "yx0")
    arrive("zx2")
    gather_y(2)

    @pl.loop(0, 5)
    def _(q):
        ad[q] = product(zd[OWN], yd[q], TN)

    arrive("zx1")
    gather_y(1)
    arrive("zx0")
    gather_y(0)
    send("y00", "y01", "y3", "y4")

    ad[OWN] = product(zd[OWN], yd[OWN], TN)

    @pl.loop(0, 5)
    def _(q):
        an[q] = product(zd[q], yd[OWN], TN)

    def gather_a(q):
        ad[OWN] += product(zx[q], yx[q], TN)

    def other_a(q):
        an[q] = keep(an[q] + product(zr[q], yx[q], TN), [n_has[q * 4 + k] for k in range(4)])

    def finish_a(q):
        ad[q] = keep(ad[q] + product(zx[q], yr[q], TN), own_flags(q))
        wd[q] = product(zd[OWN], ad[q], NN)

    for q in (3, 4):
        arrive(f"yx{q}")
        gather_a(q)
        other_a(q)
    for q in (3, 4):
        arrive(f"y{q}")
        finish_a(q)
    for q in (2, 1):
        arrive(f"yx{q}")
        gather_a(q)
        other_a(q)
    arrive("yx0")
    gather_a(0)
    send("a00", "a01", "a3", "a4")
    other_a(0)
    arrive("y00")
    send("y10", "y20")

    wd[OWN] = product(zd[OWN], ad[OWN], NN)

    @pl.loop(0, 5)
    def _(q):
        wd[OWN] += product(zd[q], an[q], NN)

    arrive("y01")
    send("y11", "y21")
    finish_a(0)

    @pl.loop(0, 5)
    def _(q):
        fd[q] = product(wd[OWN], zx[q], NT)

    fd[OWN] = product(wd[OWN], zd[OWN], NT)
    arrive("a00")
    send("a10", "a20")
    arrive("y10", "y11")
    finish_a(1)
    arrive("y20", "y21")
    finish_a(2)

    def collect(dense, out):
        for r in range(2):
            for s in range(SLOTS):
                place = o_at[r * SLOTS + s]
                both = dense[lax.div(place, 2), r * BLK : (r + 1) * BLK]
                out[r * SLOTS + s] = jnp.where(lax.rem(place, 2) > 0, both[:, BLK:], both[:, :BLK])

    def finish_f(q):
        w = keep(wd[q] + product(zd[q], ar[q], NN), own_flags(q))
        fd[OWN] += product(w, zd[q], NT)
        fd[q] += product(w, zr[q], NT)

    arrive("a01")
    send("a11", "a21")
    collect(ad, ox)
    store_x = pltpu.make_async_copy(ox, ox_hbm, local_sem.at[2])
    store_x.start()
    arrive("a3")
    finish_f(3)
    arrive("a4")
    finish_f(4)
    finish_f(0)
    arrive("a10", "a11")
    finish_f(1)
    arrive("a20", "a21")
    finish_f(2)
    collect(fd, of)
    store_f = pltpu.make_async_copy(of, of_hbm, local_sem.at[3])
    store_f.start()
    for one in c.values():
        one.wait_send()
    store_x.wait()
    store_f.wait()


def shards(z_factor, z_columns, p_columns, d_density):
    tiles = (2 * SLOTS, BLK, BLK)
    wide = (WIDE, WIDE)
    f32 = jnp.float32
    counts = [6, 6, 5, 5, 6, 5, 5, 6, 5, 5, 6, 6]
    out_x, out_f = pl.pallas_call(
        kernel,
        out_shape=[jax.ShapeDtypeStruct(tiles, f32)] * 2,
        in_specs=[pl.BlockSpec(memory_space=pltpu.HBM)] * 4,
        out_specs=[pl.BlockSpec(memory_space=pl.ANY)] * 2,
        scratch_shapes=[pltpu.VMEM(tiles, f32)] * 4
        + [pltpu.VMEM((n,) + wide, f32) for n in counts]
        + [pltpu.SMEM((SLOTS, ROWS), jnp.int32)] * 2
        + [pltpu.SMEM((n,), jnp.int32) for n in (24, 24, 24, 24, 16, 20)]
        + [pltpu.SemaphoreType.DMA((6,)), pltpu.SemaphoreType.DMA((31,)), pltpu.SemaphoreType.DMA((31,))],
        compiler_params=pltpu.CompilerParams(collective_id=0, has_side_effects=True, vmem_limit_bytes=48 * 1024 * 1024),
    )(*(pltpu.with_memory_space_constraint(x, pltpu.HBM) for x in (z_columns.T, p_columns.T, z_factor.reshape(tiles), d_density.reshape(tiles))))
    shape = z_factor.shape
    return out_x.reshape(shape), out_f.reshape(shape)


def solution(mesh):
    spec = P(("gx", "gy", "gz"), None, None, None)
    return jax.shard_map(shards, mesh=mesh, in_specs=(spec, P(), P(), spec), out_specs=(spec, spec), check_vma=False)
```

```python
import jax
import jax.numpy as jnp
from jax import lax
from jax.experimental import pallas as pl
from jax.experimental.pallas import tpu as pltpu
from jax.sharding import PartitionSpec as P

MESH = pl.DeviceIdType.MESH
BLK = 128
WIDE = 256
SLOTS = 8
GX, GY, GZ = 16, 8, 2
ROWS = 512
OWN = 5
NN = (((1,), (0,)), ((), ()))
TN = (((0,), (0,)), ((), ()))
NT = (((1,), (1,)), ((), ()))


def split(x):
    hi = x.astype(jnp.bfloat16)
    return hi, (x - hi.astype(jnp.float32)).astype(jnp.bfloat16)


def product(a, b, dims):
    a_hi, a_lo = split(a)
    b_hi, b_lo = split(b)

    def dot(x, y):
        return lax.dot_general(x, y, dims, preferred_element_type=jnp.float32)

    return dot(a_hi, b_hi) + (dot(a_hi, b_lo) + dot(a_lo, b_hi))


def kernel(
    zc_hbm, pc_hbm, z_hbm, d_hbm, ox_hbm, of_hbm,
    z_in, d_in, ox, of, zd, dd, zr, zx, yd, yr, yx, ad, ar, an, wd, fd, pd, pr, sr, rd, rr, via, qd, ur,
    z_cols, p_cols, z_at, z_has, p_at, p_has, o_at, n_has,
    local_sem, send_sem, recv_sem,
):
    gx, gy, gz = lax.axis_index("gx"), lax.axis_index("gy"), lax.axis_index("gz")
    sx = 1 - 2 * lax.rem(gx, 2)
    sy = 1 - 2 * lax.rem(gy, 2)
    near = (gx + sx, gy, gz)
    far = (lax.rem(gx - sx + GX, GX), gy, gz)
    over = (gx, gy, 1 - gz)
    core = (gx, gy + sy, gz)
    side = (gx, lax.rem(gy - sy + GY, GY), gz)
    to_z = (lax.rem(gx + 2 * sx + GX, GX), gy, gz)
    from_z = (lax.rem(gx - 2 * sx + GX, GX), gy, gz)
    cross = (gx + sx, gy, 1 - gz)

    def box(where):
        return (where[0] * GY + where[1]) * GZ + where[2]

    boxes = [box(w) for w in (near, far, over, core, side, (gx, gy, gz))]

    load_z = pltpu.make_async_copy(z_hbm, z_in, local_sem.at[0])
    load_d = pltpu.make_async_copy(d_hbm, d_in, local_sem.at[1])
    load_zc = pltpu.make_async_copy(zc_hbm, z_cols, local_sem.at[4])
    load_pc = pltpu.make_async_copy(pc_hbm, p_cols, local_sem.at[5])
    load_zc.start()
    load_z.start()
    load_pc.start()
    load_d.start()

    barrier = pltpu.get_barrier_semaphore()
    for where in (near, far, over, core, side, from_z, to_z, cross):
        pl.semaphore_signal(barrier, inc=1, device_id=where, device_id_type=MESH)

    def table(cols, at, has):
        for r in range(2):
            row = boxes[OWN] * 2 + r
            found = [cols[s, row] for s in range(SLOTS)]
            for q in (5, 2, 1, 0, 3, 4):
                for c in range(2):
                    target = boxes[q] * 2 + c
                    slot, hit = jnp.int32(0), jnp.int32(0)
                    for s in range(SLOTS):
                        same = found[s] == target
                        slot = jnp.where(same, s, slot)
                        hit = jnp.where(same, 1, hit)
                    at[r * 12 + q * 2 + c] = slot
                    has[r * 12 + q * 2 + c] = hit

    def spread(blocks, at, has, dense, q):
        for r in range(2):
            for c in range(2):
                i = r * 12 + q * 2 + c
                block = blocks[r * SLOTS + at[i]]
                dense[q, r * BLK : (r + 1) * BLK, c * BLK : (c + 1) * BLK] = jnp.where(has[i] > 0, block, 0.0)

    def keep(x, flags):
        halves = [
            jnp.concatenate([jnp.where(flags[2 * r + c] > 0, x[r * BLK : (r + 1) * BLK, c * BLK : (c + 1) * BLK], 0.0) for c in range(2)], axis=1)
            for r in range(2)
        ]
        return jnp.concatenate(halves, axis=0)

    def own_flags(q):
        return [p_has[r * 12 + q * 2 + c] for r in range(2) for c in range(2)]

    def copy(i, src, dst, where):
        return pltpu.make_async_remote_copy(
            src_ref=src, dst_ref=dst, send_sem=send_sem.at[i], recv_sem=recv_sem.at[i], device_id=where, device_id_type=MESH
        )

    load_zc.wait()
    table(z_cols, z_at, z_has)
    load_z.wait()
    spread(z_in, z_at, z_has, zd, OWN)
    pl.semaphore_wait(barrier, 8)

    c = {}

    def message(name, src, dst, where):
        c[name] = copy(len(c), src, dst, where)

    half = [pl.ds(0, BLK), pl.ds(BLK, BLK)]
    message("z0", zd.at[OWN], zr.at[0], near)
    for q, where in ((3, core), (4, side)):
        message(f"z{q}", zd.at[OWN], zr.at[q], where)
        message(f"zx{q}", zd.at[q], zx.at[q], where)
        message(f"y{q}", yd.at[OWN], yr.at[q], where)
        message(f"a{q}", ad.at[OWN], ar.at[q], where)
        message(f"yx{q}", yd.at[q], yx.at[q - 3], where)
    message("zx0", zd.at[0], zx.at[0], near)
    message("s", pd.at[0], sr, near)
    message("u", qd, ur, near)
    for q, where, back in ((1, to_z, from_z), (2, cross, cross)):
        message(f"z{q}", zr.at[0], zr.at[q], where)
        message(f"via{q}", zd.at[q], via.at[q - 1], near)
        message(f"zx{q}", via.at[q - 1], zx.at[q], where)
        message(f"p{q}", pd.at[q], pr.at[q - 1], back)
        message(f"r{q}", rd.at[q], rr.at[q - 1], back)
    for h in range(2):
        message(f"y0{h}", yd.at[OWN, half[h]], yr.at[0, half[h]], near)
        message(f"a0{h}", ad.at[OWN, half[h]], ar.at[0, half[h]], near)
        for q, where in ((1, to_z), (2, cross)):
            message(f"y{q}{h}", yr.at[0, half[h]], yr.at[q, half[h]], where)
            message(f"a{q}{h}", ar.at[0, half[h]], ar.at[q, half[h]], where)

    def send(*names):
        for name in names:
            c[name].start()

    def arrive(*names):
        for name in names:
            c[name].wait_recv()

    def tables():
        table(p_cols, p_at, p_has)
        for r in range(2):
            row = boxes[OWN] * 2 + r
            for s in range(SLOTS):
                column = p_cols[s, row]
                place = jnp.int32(0)
                for q in range(6):
                    for k in range(2):
                        place = jnp.where(column == boxes[q] * 2 + k, q * 2 + k, place)
                o_at[r * SLOTS + s] = place
        own, near_box = boxes[OWN], boxes[0]
        for q, rows, columns in ((0, box(to_z), near_box), (1, box(cross), near_box), (3, boxes[3], own), (4, boxes[4], own)):
            for r in range(2):
                found = [p_cols[s, rows * 2 + r] for s in range(SLOTS)]
                for k in range(2):
                    hit = jnp.int32(0)
                    for s in range(SLOTS):
                        hit = jnp.where(found[s] == columns * 2 + k, 1, hit)
                    n_has[q * 4 + r * 2 + k] = hit

    send("z0", "z3", "z4")
    for q, name in ((3, "zx3"), (4, "zx4"), (1, "via1"), (2, "via2"), (0, "zx0")):
        spread(z_in, z_at, z_has, zd, q)
        send(name)

    load_pc.wait()
    tables()
    load_d.wait()
    for q in (5, 3, 4, 0, 2, 1):
        spread(d_in, p_at, p_has, dd, q)

    @pl.loop(0, 6)
    def _(q):
        yd[q] = product(dd[OWN], zd[q], NN)

    def finish_y(q):
        yd[q] = keep(yd[q] + product(dd[q], zr[q], NN), own_flags(q))

    def gather_y(q):
        yd[OWN] += product(dd[q], zx[q], NN)

    arrive("z3")
    finish_y(3)
    send("yx3")
    arrive("z4")
    finish_y(4)
    send("yx4")
    def offer(q):
        pd[q] = product(zd[q], yd[q], TN)

    arrive("z0")
    send("z1", "z2")
    finish_y(0)
    offer(0)
    arrive("zx3")
    gather_y(3)
    arrive("zx4")
    gather_y(4)
    arrive("via1")
    send("zx1")
    arrive("z1")
    finish_y(1)
    offer(1)
    send("p1")
    arrive("z2")
    finish_y(2)
    offer(2)
    send("p2")

    @pl.loop(0, 5)
    def _(q):
        rd[q] = product(zd[OWN], yd[q], TN)

    send("r1")
    arrive("via2")
    send("zx2", "r2")
    arrive("zx1")
    gather_y(1)
    arrive("p1", "p2")
    pd[0] += pr[0] + pr[1]
    send("s")
    arrive("zx0")
    gather_y(0)
    arrive("zx2")
    gather_y(2)
    send("y00", "y01", "y3", "y4")

    ad[OWN] = product(zd[OWN], yd[OWN], TN)
    for q in (3, 4):
        arrive(f"yx{q}")
        ad[OWN] += product(zx[q], yx[q - 3], TN)
        x = product(zr[q], yx[q - 3], TN) + product(zd[q], yd[OWN], TN)
        an[q - 3] = keep(x, [n_has[q * 4 + k] for k in range(4)])
    arrive("s")
    ad[OWN] += sr[...]
    send("a00", "a01", "a3", "a4")

    def finish_a(q):
        ad[q] = keep(rd[q] + product(zx[q], yr[q], TN), own_flags(q))

    def finish_w(q):
        wd[q] = product(zd[OWN], ad[q], NN)

    for q in (3, 4):
        arrive(f"y{q}")
        finish_a(q)
        finish_w(q)
    wd[OWN] = product(zd[OWN], ad[OWN], NN) + (product(zd[3], an[0], NN) + product(zd[4], an[1], NN))
    arrive("r1", "r2")
    for h in range(2):
        arrive(f"y0{h}")
        send(f"y1{h}", f"y2{h}")
    finish_a(0)
    qd[...] = product(zx[0], ad[0], NN)
    for k in range(2):
        x = keep(rr[k] + product(via[k], yr[0], TN), [n_has[k * 4 + i] for i in range(4)])
        qd[...] += product(via[k], x, NN)
    send("u")
    fd[OWN] = jnp.zeros((WIDE, WIDE), jnp.float32)

    def start_f(q):
        w = keep(wd[q] + product(zd[q], ar[q], NN), own_flags(q))
        fd[OWN] += product(w, zd[q], NT)
        fd[q] = product(w, zr[q], NT)

    arrive("a3")
    start_f(3)
    arrive("a00")
    send("a10", "a20")
    arrive("a4")
    start_f(4)
    for q in (1, 2):
        arrive(f"y{q}0", f"y{q}1")
        finish_a(q)
    arrive("a01")
    send("a11", "a21")
    for q in (0, 1, 2):
        finish_w(q)
    start_f(0)

    def collect(dense, out):
        for r in range(2):
            for s in range(SLOTS):
                place = o_at[r * SLOTS + s]
                both = dense[lax.div(place, 2), r * BLK : (r + 1) * BLK]
                out[r * SLOTS + s] = jnp.where(lax.rem(place, 2) > 0, both[:, BLK:], both[:, :BLK])

    collect(ad, ox)
    store_x = pltpu.make_async_copy(ox, ox_hbm, local_sem.at[2])
    store_x.start()
    for q in (1, 2):
        arrive(f"a{q}0", f"a{q}1")
        start_f(q)
    arrive("u")
    wd[OWN] += ur[...]

    @pl.loop(0, 5)
    def _(q):
        fd[q] += product(wd[OWN], zx[q], NT)

    fd[OWN] += product(wd[OWN], zd[OWN], NT)
    collect(fd, of)
    store_f = pltpu.make_async_copy(of, of_hbm, local_sem.at[3])
    store_f.start()
    for one in c.values():
        one.wait_send()
    store_x.wait()
    store_f.wait()


def shards(z_factor, z_columns, p_columns, d_density):
    tiles = (2 * SLOTS, BLK, BLK)
    wide = (WIDE, WIDE)
    f32 = jnp.float32
    counts = [6, 6, 5, 5, 6, 5, 2, 6, 5, 2, 6, 6, 3, 2, 0, 5, 2, 2, 0, 0]
    out_x, out_f = pl.pallas_call(
        kernel,
        out_shape=[jax.ShapeDtypeStruct(tiles, f32)] * 2,
        in_specs=[pl.BlockSpec(memory_space=pltpu.HBM)] * 4,
        out_specs=[pl.BlockSpec(memory_space=pl.ANY)] * 2,
        scratch_shapes=[pltpu.VMEM(tiles, f32)] * 4
        + [pltpu.VMEM((n,) + wide if n else wide, f32) for n in counts]
        + [pltpu.SMEM((SLOTS, ROWS), jnp.int32)] * 2
        + [pltpu.SMEM((n,), jnp.int32) for n in (24, 24, 24, 24, 16, 20)]
        + [pltpu.SemaphoreType.DMA((36,)), pltpu.SemaphoreType.DMA((36,)), pltpu.SemaphoreType.DMA((37,))],
        compiler_params=pltpu.CompilerParams(collective_id=0, has_side_effects=True, vmem_limit_bytes=48 * 1024 * 1024),
    )(*(pltpu.with_memory_space_constraint(x, pltpu.HBM) for x in (z_columns.T, p_columns.T, z_factor.reshape(tiles), d_density.reshape(tiles))))
    shape = z_factor.shape
    return out_x.reshape(shape), out_f.reshape(shape)


def solution(mesh):
    spec = P(("gx", "gy", "gz"), None, None, None)
    return jax.shard_map(shards, mesh=mesh, in_specs=(spec, P(), P(), spec), out_specs=(spec, spec), check_vma=False)
```

```python
import jax
import jax.numpy as jnp
from jax import lax
from jax.experimental import pallas as pl
from jax.experimental.pallas import tpu as pltpu
from jax.sharding import PartitionSpec as P

MESH = pl.DeviceIdType.MESH
BLK = 128
WIDE = 256
SLOTS = 8
GX, GY, GZ = 16, 8, 2
ROWS = 512
CUT_Z, CUT_V, CUT = 1, 1, 4
OWN = 5
NN = (((1,), (0,)), ((), ()))
TN = (((0,), (0,)), ((), ()))
NT = (((1,), (1,)), ((), ()))


def split(x):
    hi = x.astype(jnp.bfloat16)
    return hi, (x - hi.astype(jnp.float32)).astype(jnp.bfloat16)


def product(a, b, dims):
    a_hi, a_lo = a if isinstance(a, tuple) else split(a)
    b_hi, b_lo = b if isinstance(b, tuple) else split(b)

    def dot(x, y):
        return lax.dot_general(x, y, dims, preferred_element_type=jnp.float32)

    return dot(a_hi, b_hi) + (dot(a_hi, b_lo) + dot(a_lo, b_hi))


def kernel(
    zc_hbm, pc_hbm, z_hbm, d_hbm, ox_hbm, of_hbm,
    z_in, d_in, ox, of, zd, dd, zr, zx, yd, yr, yx, ad, ar, an, wd, fd, pd, pr, sr, rd, rr, via, qd, ur,
    zd_hi, zd_lo, zx_hi, zx_lo, w_hi, w_lo,
    z_cols, p_cols, z_at, z_has, p_at, p_has, o_at, n_has,
    local_sem, send_sem, recv_sem,
):
    gx, gy, gz = lax.axis_index("gx"), lax.axis_index("gy"), lax.axis_index("gz")
    sx = 1 - 2 * lax.rem(gx, 2)
    sy = 1 - 2 * lax.rem(gy, 2)
    near = (gx + sx, gy, gz)
    far = (lax.rem(gx - sx + GX, GX), gy, gz)
    over = (gx, gy, 1 - gz)
    core = (gx, gy + sy, gz)
    side = (gx, lax.rem(gy - sy + GY, GY), gz)
    to_z = (lax.rem(gx + 2 * sx + GX, GX), gy, gz)
    from_z = (lax.rem(gx - 2 * sx + GX, GX), gy, gz)
    cross = (gx + sx, gy, 1 - gz)

    def box(where):
        return (where[0] * GY + where[1]) * GZ + where[2]

    boxes = [box(w) for w in (near, far, over, core, side, (gx, gy, gz))]

    load_z = pltpu.make_async_copy(z_hbm, z_in, local_sem.at[0])
    load_d = pltpu.make_async_copy(d_hbm, d_in, local_sem.at[1])
    load_zc = pltpu.make_async_copy(zc_hbm, z_cols, local_sem.at[4])
    load_pc = pltpu.make_async_copy(pc_hbm, p_cols, local_sem.at[5])
    load_zc.start()
    load_z.start()
    load_pc.start()
    load_d.start()

    barrier = pltpu.get_barrier_semaphore()
    for where in (near, far, over, core, side, from_z, to_z, cross):
        pl.semaphore_signal(barrier, inc=1, device_id=where, device_id_type=MESH)

    def table(cols, at, has):
        for r in range(2):
            row = boxes[OWN] * 2 + r
            found = [cols[s, row] for s in range(SLOTS)]
            for q in (5, 2, 1, 0, 3, 4):
                for c in range(2):
                    target = boxes[q] * 2 + c
                    slot, hit = jnp.int32(0), jnp.int32(0)
                    for s in range(SLOTS):
                        same = found[s] == target
                        slot = jnp.where(same, s, slot)
                        hit = jnp.where(same, 1, hit)
                    at[r * 12 + q * 2 + c] = slot
                    has[r * 12 + q * 2 + c] = hit

    def spread(blocks, at, has, dense, q):
        for r in range(2):
            for c in range(2):
                i = r * 12 + q * 2 + c
                block = blocks[r * SLOTS + at[i]]
                dense[q, r * BLK : (r + 1) * BLK, c * BLK : (c + 1) * BLK] = jnp.where(has[i] > 0, block, 0.0)

    def keep(x, flags):
        halves = [
            jnp.concatenate([jnp.where(flags[2 * r + c] > 0, x[r * BLK : (r + 1) * BLK, c * BLK : (c + 1) * BLK], 0.0) for c in range(2)], axis=1)
            for r in range(2)
        ]
        return jnp.concatenate(halves, axis=0)

    def own_flags(q):
        return [p_has[r * 12 + q * 2 + c] for r in range(2) for c in range(2)]

    def copy(i, src, dst, where):
        return pltpu.make_async_remote_copy(
            src_ref=src, dst_ref=dst, send_sem=send_sem.at[i], recv_sem=recv_sem.at[i], device_id=where, device_id_type=MESH
        )

    load_zc.wait()
    table(z_cols, z_at, z_has)
    load_z.wait()
    spread(z_in, z_at, z_has, zd, OWN)
    pl.semaphore_wait(barrier, 8)

    c = {}

    def message(name, src, dst, where):
        c[name] = copy(len(c), src, dst, where)

    def parts(name, count, src, dst, where):
        rows = WIDE // count
        for h in range(count):
            part = pl.ds(h * rows, rows)
            message(f"{name}{h}", src.at[part], dst.at[part], where)

    parts("z0", CUT_Z, zd.at[OWN], zr.at[0], near)
    for q, where in ((3, core), (4, side)):
        message(f"z{q}", zd.at[OWN], zr.at[q], where)
        message(f"zx{q}", zd.at[q], zx.at[q], where)
        message(f"y{q}", yd.at[OWN], yr.at[q], where)
        message(f"a{q}", ad.at[OWN], ar.at[q], where)
        message(f"yx{q}", yd.at[q], yx.at[q - 3], where)
    message("zx0", zd.at[0], zx.at[0], near)
    message("s", pd.at[0], sr, near)
    message("u", qd, ur, near)
    parts("y0", CUT, yd.at[OWN], yr.at[0], near)
    parts("a0", CUT, ad.at[OWN], ar.at[0], near)
    for q, where, back in ((1, to_z, from_z), (2, cross, cross)):
        parts(f"z{q}", CUT_Z, zr.at[0], zr.at[q], where)
        parts(f"via{q}", CUT_V, zd.at[q], via.at[q - 1], near)
        parts(f"zx{q}", CUT_V, via.at[q - 1], zx.at[q], where)
        message(f"p{q}", pd.at[q], pr.at[q - 1], back)
        message(f"r{q}", rd.at[q], rr.at[q - 1], back)
        parts(f"y{q}", CUT, yr.at[0], yr.at[q], where)
        parts(f"a{q}", CUT, ar.at[0], ar.at[q], where)

    def send(*names):
        for name in names:
            c[name].start()

    def arrive(*names):
        for name in names:
            c[name].wait_recv()

    def all_of(name, count):
        return [f"{name}{h}" for h in range(count)]

    def relay(name, count, *onward):
        for h in range(count):
            arrive(f"{name}{h}")
            send(*(f"{other}{h}" for other in onward))

    def tables():
        table(p_cols, p_at, p_has)
        for r in range(2):
            row = boxes[OWN] * 2 + r
            for s in range(SLOTS):
                column = p_cols[s, row]
                place = jnp.int32(0)
                for q in range(6):
                    for k in range(2):
                        place = jnp.where(column == boxes[q] * 2 + k, q * 2 + k, place)
                o_at[r * SLOTS + s] = place
        own, near_box = boxes[OWN], boxes[0]
        for q, rows, columns in ((0, box(to_z), near_box), (1, box(cross), near_box), (3, boxes[3], own), (4, boxes[4], own)):
            for r in range(2):
                found = [p_cols[s, rows * 2 + r] for s in range(SLOTS)]
                for k in range(2):
                    hit = jnp.int32(0)
                    for s in range(SLOTS):
                        hit = jnp.where(found[s] == columns * 2 + k, 1, hit)
                    n_has[q * 4 + r * 2 + k] = hit

    send("z3", "z4", *all_of("z0", CUT_Z))
    for q, name in ((3, "zx3"), (4, "zx4"), (1, "via1"), (2, "via2"), (0, "zx0")):
        spread(z_in, z_at, z_has, zd, q)
        send(*(all_of(name, CUT_V) if q in (1, 2) else [name]))

    load_pc.wait()
    tables()
    load_d.wait()
    for q in (5, 3, 4, 0, 2, 1):
        spread(d_in, p_at, p_has, dd, q)

    def own_z(q):
        return zd_hi[q], zd_lo[q]

    def near_z(q):
        return zx_hi[q], zx_lo[q]

    @pl.loop(0, 6)
    def _(q):
        zd_hi[q], zd_lo[q] = split(zd[q])
        yd[q] = product(dd[OWN], own_z(q), NN)

    def finish_y(q):
        yd[q] = keep(yd[q] + product(dd[q], zr[q], NN), own_flags(q))

    def gather_y(q):
        zx_hi[q], zx_lo[q] = split(zx[q])
        yd[OWN] += product(dd[q], near_z(q), NN)

    arrive("z3")
    finish_y(3)
    send("yx3")
    arrive("z4")
    finish_y(4)
    send("yx4")
    def offer(q):
        pd[q] = product(own_z(q), yd[q], TN)

    relay("z0", CUT_Z, "z1", "z2")
    finish_y(0)
    offer(0)
    arrive("zx3")
    gather_y(3)
    arrive("zx4")
    gather_y(4)
    relay("via1", CUT_V, "zx1")
    arrive(*all_of("z1", CUT_Z))
    finish_y(1)
    offer(1)
    send("p1")
    arrive(*all_of("z2", CUT_Z))
    finish_y(2)
    offer(2)
    send("p2")

    @pl.loop(0, 5)
    def _(q):
        rd[q] = product(own_z(OWN), yd[q], TN)

    send("r1")
    relay("via2", CUT_V, "zx2")
    send("r2")
    arrive(*all_of("zx1", CUT_V))
    gather_y(1)
    arrive("p1", "p2")
    pd[0] += pr[0] + pr[1]
    send("s")
    arrive("zx0")
    gather_y(0)
    arrive(*all_of("zx2", CUT_V))
    gather_y(2)
    send(*all_of("y0", CUT), "y3", "y4")

    ad[OWN] = product(own_z(OWN), yd[OWN], TN)
    for q in (3, 4):
        arrive(f"yx{q}")
        ad[OWN] += product(near_z(q), yx[q - 3], TN)
        x = product(zr[q], yx[q - 3], TN) + product(own_z(q), yd[OWN], TN)
        an[q - 3] = keep(x, [n_has[q * 4 + k] for k in range(4)])
    arrive("s")
    ad[OWN] += sr[...]
    send(*all_of("a0", CUT), "a3", "a4")

    def finish_a(q):
        ad[q] = keep(rd[q] + product(near_z(q), yr[q], TN), own_flags(q))

    def finish_w(q):
        wd[q] = product(own_z(OWN), ad[q], NN)

    for q in (3, 4):
        arrive(f"y{q}")
        finish_a(q)
        finish_w(q)
    wd[OWN] = product(own_z(OWN), ad[OWN], NN) + (product(zd[3], an[0], NN) + product(zd[4], an[1], NN))
    arrive("r1", "r2")
    relay("y0", CUT, "y1", "y2")
    hop = [split(via[k]) for k in range(2)]
    y_near = split(yr[0])
    raw = [product(near_z(0), y_near, TN)] + [product(hop[k], y_near, TN) for k in range(2)]
    x0 = keep(rd[0] + raw[0], own_flags(0))
    x1, x2 = (keep(rr[k] + raw[k + 1], [n_has[k * 4 + i] for i in range(4)]) for k in range(2))
    qd[...] = product(near_z(0), x0, NN) + product(hop[0], x1, NN) + product(hop[1], x2, NN)
    send("u")
    ad[0] = x0
    fd[OWN] = jnp.zeros((WIDE, WIDE), jnp.float32)

    def start_f(*qs):
        raw = [product(own_z(q), ar[q], NN) for q in qs]
        ws = [split(keep(wd[q] + x, own_flags(q))) for q, x in zip(qs, raw)]
        for q, w in zip(qs, ws):
            fd[q] = product(w, zr[q], NT)
        own = [product(w, own_z(q), NT) for q, w in zip(qs, ws)]
        fd[OWN] += own[0] if len(qs) == 1 else own[0] + own[1]

    relay("a0", CUT, "a1", "a2")
    arrive("a3", "a4")
    start_f(3, 4)
    for q in (1, 2):
        arrive(*all_of(f"y{q}", CUT))
        finish_a(q)
    for q in (0, 1, 2):
        finish_w(q)
    start_f(0)

    def collect(dense, out):
        for r in range(2):
            for s in range(SLOTS):
                place = o_at[r * SLOTS + s]
                both = dense[lax.div(place, 2), r * BLK : (r + 1) * BLK]
                out[r * SLOTS + s] = jnp.where(lax.rem(place, 2) > 0, both[:, BLK:], both[:, :BLK])

    collect(ad, ox)
    store_x = pltpu.make_async_copy(ox, ox_hbm, local_sem.at[2])
    store_x.start()
    arrive(*all_of("a1", CUT), *all_of("a2", CUT))
    start_f(1, 2)
    arrive("u")
    w_hi[...], w_lo[...] = split(wd[OWN] + ur[...])

    @pl.loop(0, 5, unroll=5)
    def _(q):
        fd[q] += product((w_hi[...], w_lo[...]), near_z(q), NT)

    fd[OWN] += product((w_hi[...], w_lo[...]), own_z(OWN), NT)
    collect(fd, of)
    store_f = pltpu.make_async_copy(of, of_hbm, local_sem.at[3])
    store_f.start()
    for one in c.values():
        one.wait_send()
    store_x.wait()
    store_f.wait()


def shards(z_factor, z_columns, p_columns, d_density):
    tiles = (2 * SLOTS, BLK, BLK)
    wide = (WIDE, WIDE)
    f32 = jnp.float32
    counts = [6, 6, 5, 5, 6, 5, 2, 6, 5, 2, 6, 6, 3, 2, 0, 5, 2, 2, 0, 0]
    out_x, out_f = pl.pallas_call(
        kernel,
        out_shape=[jax.ShapeDtypeStruct(tiles, f32)] * 2,
        in_specs=[pl.BlockSpec(memory_space=pltpu.HBM)] * 4,
        out_specs=[pl.BlockSpec(memory_space=pl.ANY)] * 2,
        scratch_shapes=[pltpu.VMEM(tiles, f32)] * 4
        + [pltpu.VMEM((n,) + wide if n else wide, f32) for n in counts]
        + [pltpu.VMEM((n,) + wide if n else wide, jnp.bfloat16) for n in (6, 6, 5, 5, 0, 0)]
        + [pltpu.SMEM((SLOTS, ROWS), jnp.int32)] * 2
        + [pltpu.SMEM((n,), jnp.int32) for n in (24, 24, 24, 24, 16, 20)]
        + [pltpu.SemaphoreType.DMA((6,)), pltpu.SemaphoreType.DMA((48,)), pltpu.SemaphoreType.DMA((48,))],
        compiler_params=pltpu.CompilerParams(collective_id=0, has_side_effects=True, vmem_limit_bytes=48 * 1024 * 1024),
    )(*(pltpu.with_memory_space_constraint(x, pltpu.HBM) for x in (z_columns.T, p_columns.T, z_factor.reshape(tiles), d_density.reshape(tiles))))
    shape = z_factor.shape
    return out_x.reshape(shape), out_f.reshape(shape)


def solution(mesh):
    spec = P(("gx", "gy", "gz"), None, None, None)
    return jax.shard_map(shards, mesh=mesh, in_specs=(spec, P(), P(), spec), out_specs=(spec, spec), check_vma=False)
```

```python
import jax
import jax.numpy as jnp
from jax import lax
from jax.experimental import pallas as pl
from jax.experimental.pallas import tpu as pltpu
from jax.sharding import PartitionSpec as P

MESH = pl.DeviceIdType.MESH
BLK = 128
WIDE = 256
SLOTS = 8
GX, GY, GZ = 16, 8, 2
ROWS = 512
CUT_Z, CUT_V, CUT = 1, 1, 4
OWN = 5
NN = (((1,), (0,)), ((), ()))
TN = (((0,), (0,)), ((), ()))
NT = (((1,), (1,)), ((), ()))


def split(x):
    hi = x.astype(jnp.bfloat16)
    return hi, (x - hi.astype(jnp.float32)).astype(jnp.bfloat16)


def product(a, b, dims):
    a_hi, a_lo = a if isinstance(a, tuple) else split(a)
    b_hi, b_lo = b if isinstance(b, tuple) else split(b)

    def dot(x, y):
        return lax.dot_general(x, y, dims, preferred_element_type=jnp.float32)

    return dot(a_hi, b_hi) + (dot(a_hi, b_lo) + dot(a_lo, b_hi))


def kernel(
    zc_hbm, pc_hbm, z_hbm, d_hbm, ox, of,
    z_in, d_in, zd, dd, zr, zx, yd, yr, yx, ad, ar, an, wd, fd, pd, pr, sr, rd, rr, via, qd, ur,
    zd_hi, zd_lo, zx_hi, zx_lo, w_hi, w_lo,
    z_cols, p_cols, z_at, z_has, p_at, p_has, o_at, n_has,
    local_sem, send_sem, recv_sem,
):
    gx, gy, gz = lax.axis_index("gx"), lax.axis_index("gy"), lax.axis_index("gz")
    sx = 1 - 2 * lax.rem(gx, 2)
    sy = 1 - 2 * lax.rem(gy, 2)
    near = (gx + sx, gy, gz)
    far = (lax.rem(gx - sx + GX, GX), gy, gz)
    over = (gx, gy, 1 - gz)
    core = (gx, gy + sy, gz)
    side = (gx, lax.rem(gy - sy + GY, GY), gz)
    to_z = (lax.rem(gx + 2 * sx + GX, GX), gy, gz)
    from_z = (lax.rem(gx - 2 * sx + GX, GX), gy, gz)
    cross = (gx + sx, gy, 1 - gz)

    def box(where):
        return (where[0] * GY + where[1]) * GZ + where[2]

    boxes = [box(w) for w in (near, far, over, core, side, (gx, gy, gz))]

    load_z = pltpu.make_async_copy(z_hbm, z_in, local_sem.at[0])
    load_d = pltpu.make_async_copy(d_hbm, d_in, local_sem.at[1])
    load_zc = pltpu.make_async_copy(zc_hbm, z_cols, local_sem.at[4])
    load_pc = pltpu.make_async_copy(pc_hbm, p_cols, local_sem.at[5])
    load_zc.start()
    load_z.start()
    load_pc.start()
    load_d.start()

    barrier = pltpu.get_barrier_semaphore()
    for where in (near, far, over, core, side, from_z, to_z, cross):
        pl.semaphore_signal(barrier, inc=1, device_id=where, device_id_type=MESH)

    def table(cols, at, has):
        for r in range(2):
            row = boxes[OWN] * 2 + r
            found = [cols[s, row] for s in range(SLOTS)]
            for q in (5, 2, 1, 0, 3, 4):
                for c in range(2):
                    target = boxes[q] * 2 + c
                    slot, hit = jnp.int32(0), jnp.int32(0)
                    for s in range(SLOTS):
                        same = found[s] == target
                        slot = jnp.where(same, s, slot)
                        hit = jnp.where(same, 1, hit)
                    at[r * 12 + q * 2 + c] = slot
                    has[r * 12 + q * 2 + c] = hit

    def spread(blocks, at, has, dense, q):
        for r in range(2):
            for c in range(2):
                i = r * 12 + q * 2 + c
                block = blocks[r * SLOTS + at[i]]
                dense[q, r * BLK : (r + 1) * BLK, c * BLK : (c + 1) * BLK] = jnp.where(has[i] > 0, block, 0.0)

    def keep(x, flags):
        halves = [
            jnp.concatenate([jnp.where(flags[2 * r + c] > 0, x[r * BLK : (r + 1) * BLK, c * BLK : (c + 1) * BLK], 0.0) for c in range(2)], axis=1)
            for r in range(2)
        ]
        return jnp.concatenate(halves, axis=0)

    def own_flags(q):
        return [p_has[r * 12 + q * 2 + c] for r in range(2) for c in range(2)]

    def copy(i, src, dst, where):
        return pltpu.make_async_remote_copy(
            src_ref=src, dst_ref=dst, send_sem=send_sem.at[i], recv_sem=recv_sem.at[i], device_id=where, device_id_type=MESH
        )

    load_zc.wait()
    table(z_cols, z_at, z_has)
    load_z.wait()
    spread(z_in, z_at, z_has, zd, OWN)
    pl.semaphore_wait(barrier, 8)

    c = {}

    def message(name, src, dst, where):
        c[name] = copy(len(c), src, dst, where)

    def parts(name, count, src, dst, where):
        rows = WIDE // count
        for h in range(count):
            part = pl.ds(h * rows, rows)
            message(f"{name}{h}", src.at[part], dst.at[part], where)

    parts("z0", CUT_Z, zd.at[OWN], zr.at[0], near)
    for q, where in ((3, core), (4, side)):
        message(f"z{q}", zd.at[OWN], zr.at[q], where)
        message(f"zx{q}", zd.at[q], zx.at[q], where)
        message(f"y{q}", yd.at[OWN], yr.at[q], where)
        message(f"a{q}", ad.at[OWN], ar.at[q], where)
        message(f"yx{q}", yd.at[q], yx.at[q - 3], where)
    message("zx0", zd.at[0], zx.at[0], near)
    message("s", pd.at[0], sr, near)
    message("u", qd, ur, near)
    parts("y0", CUT, yd.at[OWN], yr.at[0], near)
    parts("a0", CUT, ad.at[OWN], ar.at[0], near)
    for q, where, back in ((1, to_z, from_z), (2, cross, cross)):
        parts(f"z{q}", CUT_Z, zr.at[0], zr.at[q], where)
        parts(f"via{q}", CUT_V, zd.at[q], via.at[q - 1], near)
        parts(f"zx{q}", CUT_V, via.at[q - 1], zx.at[q], where)
        message(f"p{q}", pd.at[q], pr.at[q - 1], back)
        message(f"r{q}", rd.at[q], rr.at[q - 1], back)
        parts(f"y{q}", CUT, yr.at[0], yr.at[q], where)
        parts(f"a{q}", CUT, ar.at[0], ar.at[q], where)

    def send(*names):
        for name in names:
            c[name].start()

    def arrive(*names):
        for name in names:
            c[name].wait_recv()

    def all_of(name, count):
        return [f"{name}{h}" for h in range(count)]

    def relay(name, count, *onward):
        for h in range(count):
            arrive(f"{name}{h}")
            send(*(f"{other}{h}" for other in onward))

    def tables():
        table(p_cols, p_at, p_has)
        for r in range(2):
            row = boxes[OWN] * 2 + r
            for s in range(SLOTS):
                column = p_cols[s, row]
                place = jnp.int32(0)
                for q in range(6):
                    for k in range(2):
                        place = jnp.where(column == boxes[q] * 2 + k, q * 2 + k, place)
                o_at[r * SLOTS + s] = place
        own, near_box = boxes[OWN], boxes[0]
        for q, rows, columns in ((0, box(to_z), near_box), (1, box(cross), near_box), (3, boxes[3], own), (4, boxes[4], own)):
            for r in range(2):
                found = [p_cols[s, rows * 2 + r] for s in range(SLOTS)]
                for k in range(2):
                    hit = jnp.int32(0)
                    for s in range(SLOTS):
                        hit = jnp.where(found[s] == columns * 2 + k, 1, hit)
                    n_has[q * 4 + r * 2 + k] = hit

    send("z3", "z4", *all_of("z0", CUT_Z))
    for q, name in ((3, "zx3"), (4, "zx4"), (1, "via1"), (2, "via2"), (0, "zx0")):
        spread(z_in, z_at, z_has, zd, q)
        send(*(all_of(name, CUT_V) if q in (1, 2) else [name]))

    load_pc.wait()
    tables()
    load_d.wait()
    for q in (5, 3, 4, 0, 2, 1):
        spread(d_in, p_at, p_has, dd, q)

    def own_z(q):
        return zd_hi[q], zd_lo[q]

    def near_z(q):
        return zx_hi[q], zx_lo[q]

    @pl.loop(0, 6)
    def _(q):
        zd_hi[q], zd_lo[q] = split(zd[q])
        yd[q] = product(dd[OWN], own_z(q), NN)

    def finish_y(q):
        yd[q] = keep(yd[q] + product(dd[q], zr[q], NN), own_flags(q))

    def gather_y(q):
        zx_hi[q], zx_lo[q] = split(zx[q])
        yd[OWN] += product(dd[q], near_z(q), NN)

    arrive("z3")
    finish_y(3)
    send("yx3")
    arrive("z4")
    finish_y(4)
    send("yx4")
    def offer(q):
        pd[q] = product(own_z(q), yd[q], TN)

    relay("z0", CUT_Z, "z1", "z2")
    finish_y(0)
    offer(0)
    arrive("zx3")
    gather_y(3)
    arrive("zx4")
    gather_y(4)
    relay("via1", CUT_V, "zx1")
    arrive(*all_of("z1", CUT_Z))
    finish_y(1)
    offer(1)
    send("p1")
    arrive(*all_of("z2", CUT_Z))
    finish_y(2)
    offer(2)
    send("p2")

    @pl.loop(0, 5)
    def _(q):
        rd[q] = product(own_z(OWN), yd[q], TN)

    send("r1")
    relay("via2", CUT_V, "zx2")
    send("r2")
    arrive(*all_of("zx1", CUT_V))
    gather_y(1)
    arrive("p1", "p2")
    pd[0] += pr[0] + pr[1]
    send("s")
    arrive("zx0")
    gather_y(0)
    arrive(*all_of("zx2", CUT_V))
    gather_y(2)
    send(*all_of("y0", CUT), "y3", "y4")

    ad[OWN] = product(own_z(OWN), yd[OWN], TN)
    for q in (3, 4):
        arrive(f"yx{q}")
        ad[OWN] += product(near_z(q), yx[q - 3], TN)
        x = product(zr[q], yx[q - 3], TN) + product(own_z(q), yd[OWN], TN)
        an[q - 3] = keep(x, [n_has[q * 4 + k] for k in range(4)])
    arrive("s")
    ad[OWN] += sr[...]
    send(*all_of("a0", CUT), "a3", "a4")

    def finish_a(q):
        ad[q] = keep(rd[q] + product(near_z(q), yr[q], TN), own_flags(q))

    def finish_w(q):
        wd[q] = product(own_z(OWN), ad[q], NN)

    for q in (3, 4):
        arrive(f"y{q}")
        finish_a(q)
        finish_w(q)
    wd[OWN] = product(own_z(OWN), ad[OWN], NN) + (product(zd[3], an[0], NN) + product(zd[4], an[1], NN))
    arrive("r1", "r2")
    relay("y0", CUT, "y1", "y2")
    hop = [split(via[k]) for k in range(2)]
    y_near = split(yr[0])
    raw = [product(near_z(0), y_near, TN)] + [product(hop[k], y_near, TN) for k in range(2)]
    x0 = keep(rd[0] + raw[0], own_flags(0))
    x1, x2 = (keep(rr[k] + raw[k + 1], [n_has[k * 4 + i] for i in range(4)]) for k in range(2))
    qd[...] = product(near_z(0), x0, NN) + product(hop[0], x1, NN) + product(hop[1], x2, NN)
    send("u")
    ad[0] = x0
    fd[OWN] = jnp.zeros((WIDE, WIDE), jnp.float32)

    def start_f(*qs):
        raw = [product(own_z(q), ar[q], NN) for q in qs]
        ws = [split(keep(wd[q] + x, own_flags(q))) for q, x in zip(qs, raw)]
        for q, w in zip(qs, ws):
            fd[q] = product(w, zr[q], NT)
        own = [product(w, own_z(q), NT) for q, w in zip(qs, ws)]
        fd[OWN] += own[0] if len(qs) == 1 else own[0] + own[1]

    relay("a0", CUT, "a1", "a2")
    arrive("a3", "a4")
    start_f(3, 4)
    for q in (1, 2):
        arrive(*all_of(f"y{q}", CUT))
        finish_a(q)
    for q in (0, 1, 2):
        finish_w(q)
    start_f(0)

    def collect(dense, out):
        for r in range(2):
            for s in range(SLOTS):
                place = o_at[r * SLOTS + s]
                both = dense[lax.div(place, 2), r * BLK : (r + 1) * BLK]
                out[r * SLOTS + s] = jnp.where(lax.rem(place, 2) > 0, both[:, BLK:], both[:, :BLK])

    collect(ad, ox)
    arrive(*all_of("a1", CUT), *all_of("a2", CUT))
    start_f(1, 2)
    arrive("u")
    w_hi[...], w_lo[...] = split(wd[OWN] + ur[...])

    @pl.loop(0, 5, unroll=5)
    def _(q):
        fd[q] += product((w_hi[...], w_lo[...]), near_z(q), NT)

    fd[OWN] += product((w_hi[...], w_lo[...]), own_z(OWN), NT)
    collect(fd, of)
    for one in c.values():
        one.wait_send()


def deliver(x, f, out_x, out_f, sem):
    copies = [pltpu.make_async_copy(x, out_x, sem.at[0]), pltpu.make_async_copy(f, out_f, sem.at[1])]
    for one in copies:
        one.start()
    for one in copies:
        one.wait()


def shards(z_factor, z_columns, p_columns, d_density):
    tiles = (2 * SLOTS, BLK, BLK)
    wide = (WIDE, WIDE)
    f32 = jnp.float32
    counts = [6, 6, 5, 5, 6, 5, 2, 6, 5, 2, 6, 6, 3, 2, 0, 5, 2, 2, 0, 0]
    out_x, out_f = pl.pallas_call(
        kernel,
        out_shape=[pltpu.VMEM(tiles, f32)] * 2,
        in_specs=[pl.BlockSpec(memory_space=pltpu.HBM)] * 4,
        out_specs=[pl.BlockSpec(memory_space=pltpu.VMEM)] * 2,
        scratch_shapes=[pltpu.VMEM(tiles, f32)] * 2
        + [pltpu.VMEM((n,) + wide if n else wide, f32) for n in counts]
        + [pltpu.VMEM((n,) + wide if n else wide, jnp.bfloat16) for n in (6, 6, 5, 5, 0, 0)]
        + [pltpu.SMEM((SLOTS, ROWS), jnp.int32)] * 2
        + [pltpu.SMEM((n,), jnp.int32) for n in (24, 24, 24, 24, 16, 20)]
        + [pltpu.SemaphoreType.DMA((6,)), pltpu.SemaphoreType.DMA((48,)), pltpu.SemaphoreType.DMA((48,))],
        compiler_params=pltpu.CompilerParams(collective_id=0, has_side_effects=True, vmem_limit_bytes=48 * 1024 * 1024),
    )(*(pltpu.with_memory_space_constraint(x, pltpu.HBM) for x in (z_columns.T, p_columns.T, z_factor.reshape(tiles), d_density.reshape(tiles))))
    out_x, out_f = pl.pallas_call(
        deliver,
        out_shape=[pltpu.HBM(tiles, f32)] * 2,
        in_specs=[pl.BlockSpec(memory_space=pltpu.VMEM)] * 2,
        out_specs=[pl.BlockSpec(memory_space=pltpu.HBM)] * 2,
        scratch_shapes=[pltpu.SemaphoreType.DMA((2,))],
    )(*(pltpu.with_memory_space_constraint(x, pltpu.VMEM) for x in (out_x, out_f)))
    shape = z_factor.shape
    return out_x.reshape(shape), out_f.reshape(shape)


def solution(mesh):
    spec = P(("gx", "gy", "gz"), None, None, None)
    return jax.shard_map(shards, mesh=mesh, in_specs=(spec, P(), P(), spec), out_specs=(spec, spec), check_vma=False)
```

```python
import jax
import jax.numpy as jnp
from jax import lax
from jax.experimental import pallas as pl
from jax.experimental.pallas import tpu as pltpu
from jax.sharding import PartitionSpec as P

MESH = pl.DeviceIdType.MESH
BLK = 128
WIDE = 256
SLOTS = 8
GX, GY, GZ = 16, 8, 2
ROWS = 512
CUT_Z, CUT_V, CUT = 1, 1, 4
OWN = 5
NN = (((1,), (0,)), ((), ()))
TN = (((0,), (0,)), ((), ()))
NT = (((1,), (1,)), ((), ()))


def split(x):
    hi = x.astype(jnp.bfloat16)
    return hi, (x - hi.astype(jnp.float32)).astype(jnp.bfloat16)


def product(a, b, dims):
    a_hi, a_lo = a if isinstance(a, tuple) else split(a)
    b_hi, b_lo = b if isinstance(b, tuple) else split(b)

    def dot(x, y):
        return lax.dot_general(x, y, dims, preferred_element_type=jnp.float32)

    return dot(a_hi, b_hi) + (dot(a_hi, b_lo) + dot(a_lo, b_hi))


def kernel(
    zc_hbm, pc_hbm, z_hbm, d_hbm, ox, of,
    z_in, d_in, zd, dd, zr, zx, yd, yr, yx, ad, ar, an, wd, fd, pd, pr, sr, rd, rr, via, qd, ur,
    zd_hi, zd_lo, zx_hi, zx_lo, w_hi, w_lo,
    z_cols, p_cols, z_at, z_has, p_at, p_has, o_at, n_has,
    local_sem, send_sem, recv_sem,
):
    gx, gy, gz = lax.axis_index("gx"), lax.axis_index("gy"), lax.axis_index("gz")
    sx = 1 - 2 * lax.rem(gx, 2)
    sy = 1 - 2 * lax.rem(gy, 2)
    near = (gx + sx, gy, gz)
    far = (lax.rem(gx - sx + GX, GX), gy, gz)
    over = (gx, gy, 1 - gz)
    core = (gx, gy + sy, gz)
    side = (gx, lax.rem(gy - sy + GY, GY), gz)
    to_z = (lax.rem(gx + 2 * sx + GX, GX), gy, gz)
    from_z = (lax.rem(gx - 2 * sx + GX, GX), gy, gz)
    cross = (gx + sx, gy, 1 - gz)

    def box(where):
        return (where[0] * GY + where[1]) * GZ + where[2]

    boxes = [box(w) for w in (near, far, over, core, side, (gx, gy, gz))]

    load_z = pltpu.make_async_copy(z_hbm, z_in, local_sem.at[0])
    load_d = pltpu.make_async_copy(d_hbm, d_in, local_sem.at[1])
    load_zc = pltpu.make_async_copy(zc_hbm, z_cols, local_sem.at[4])
    load_pc = pltpu.make_async_copy(pc_hbm, p_cols, local_sem.at[5])
    load_zc.start()
    load_z.start()
    load_pc.start()
    load_d.start()

    barrier = pltpu.get_barrier_semaphore()
    for where in (near, far, over, core, side, from_z, to_z, cross):
        pl.semaphore_signal(barrier, inc=1, device_id=where, device_id_type=MESH)

    def table(cols, at, has):
        for r in range(2):
            row = boxes[OWN] * 2 + r
            found = [cols[s, row] for s in range(SLOTS)]
            for q in (5, 2, 1, 0, 3, 4):
                for c in range(2):
                    target = boxes[q] * 2 + c
                    slot, hit = jnp.int32(0), jnp.int32(0)
                    for s in range(SLOTS):
                        same = found[s] == target
                        slot = jnp.where(same, s, slot)
                        hit = jnp.where(same, 1, hit)
                    at[r * 12 + q * 2 + c] = slot
                    has[r * 12 + q * 2 + c] = hit

    def spread(blocks, at, has, dense, q):
        for r in range(2):
            for c in range(2):
                i = r * 12 + q * 2 + c
                block = blocks[r * SLOTS + at[i]]
                dense[q, r * BLK : (r + 1) * BLK, c * BLK : (c + 1) * BLK] = jnp.where(has[i] > 0, block, 0.0)

    def keep(x, flags):
        halves = [
            jnp.concatenate([jnp.where(flags[2 * r + c] > 0, x[r * BLK : (r + 1) * BLK, c * BLK : (c + 1) * BLK], 0.0) for c in range(2)], axis=1)
            for r in range(2)
        ]
        return jnp.concatenate(halves, axis=0)

    def own_flags(q):
        return [p_has[r * 12 + q * 2 + c] for r in range(2) for c in range(2)]

    def copy(i, src, dst, where):
        return pltpu.make_async_remote_copy(
            src_ref=src, dst_ref=dst, send_sem=send_sem.at[i], recv_sem=recv_sem.at[i], device_id=where, device_id_type=MESH
        )

    load_zc.wait()
    table(z_cols, z_at, z_has)
    load_z.wait()
    spread(z_in, z_at, z_has, zd, OWN)
    pl.semaphore_wait(barrier, 8)

    c = {}

    def message(name, src, dst, where):
        c[name] = copy(len(c), src, dst, where)

    def parts(name, count, src, dst, where):
        rows = WIDE // count
        for h in range(count):
            part = pl.ds(h * rows, rows)
            message(f"{name}{h}", src.at[part], dst.at[part], where)

    parts("z0", CUT_Z, zd.at[OWN], zr.at[0], near)
    for q, where in ((3, core), (4, side)):
        message(f"z{q}", zd.at[OWN], zr.at[q], where)
        message(f"zx{q}", zd.at[q], zx.at[q], where)
        message(f"y{q}", yd.at[OWN], yr.at[q], where)
        message(f"a{q}", ad.at[OWN], ar.at[q], where)
        message(f"yx{q}", yd.at[q], yx.at[q - 3], where)
    message("zx0", zd.at[0], zx.at[0], near)
    message("s", pd.at[0], sr, near)
    message("u", qd, ur, near)
    parts("y0", CUT, yd.at[OWN], yr.at[0], near)
    parts("a0", CUT, ad.at[OWN], ar.at[0], near)
    for q, where, back in ((1, to_z, from_z), (2, cross, cross)):
        parts(f"z{q}", CUT_Z, zr.at[0], zr.at[q], where)
        parts(f"via{q}", CUT_V, zd.at[q], via.at[q - 1], near)
        parts(f"zx{q}", CUT_V, via.at[q - 1], zx.at[q], where)
        message(f"p{q}", pd.at[q], pr.at[q - 1], back)
        message(f"r{q}", rd.at[q], rr.at[q - 1], back)
        parts(f"y{q}", CUT, yr.at[0], yr.at[q], where)
        parts(f"a{q}", CUT, ar.at[0], ar.at[q], where)

    def send(*names):
        for name in names:
            c[name].start()

    def arrive(*names):
        for name in names:
            c[name].wait_recv()

    def all_of(name, count):
        return [f"{name}{h}" for h in range(count)]

    def relay(name, count, *onward):
        for h in range(count):
            arrive(f"{name}{h}")
            send(*(f"{other}{h}" for other in onward))

    def tables():
        table(p_cols, p_at, p_has)
        for r in range(2):
            row = boxes[OWN] * 2 + r
            for s in range(SLOTS):
                column = p_cols[s, row]
                place = jnp.int32(0)
                for q in range(6):
                    for k in range(2):
                        place = jnp.where(column == boxes[q] * 2 + k, q * 2 + k, place)
                o_at[r * SLOTS + s] = place
        own, near_box = boxes[OWN], boxes[0]
        for q, rows, columns in ((0, box(to_z), near_box), (1, box(cross), near_box), (3, boxes[3], own), (4, boxes[4], own)):
            for r in range(2):
                found = [p_cols[s, rows * 2 + r] for s in range(SLOTS)]
                for k in range(2):
                    hit = jnp.int32(0)
                    for s in range(SLOTS):
                        hit = jnp.where(found[s] == columns * 2 + k, 1, hit)
                    n_has[q * 4 + r * 2 + k] = hit

    send("z3", "z4", *all_of("z0", CUT_Z))
    for q, name in ((3, "zx3"), (4, "zx4"), (1, "via1"), (2, "via2"), (0, "zx0")):
        spread(z_in, z_at, z_has, zd, q)
        send(*(all_of(name, CUT_V) if q in (1, 2) else [name]))

    load_pc.wait()
    tables()
    load_d.wait()
    for q in (5, 3, 4, 0, 2, 1):
        spread(d_in, p_at, p_has, dd, q)

    def own_z(q):
        return zd_hi[q], zd_lo[q]

    def near_z(q):
        return zx_hi[q], zx_lo[q]

    @pl.loop(0, 6)
    def _(q):
        zd_hi[q], zd_lo[q] = split(zd[q])
        yd[q] = product(dd[OWN], own_z(q), NN)

    def finish_y(q):
        yd[q] = keep(yd[q] + product(dd[q], zr[q], NN), own_flags(q))

    def gather_y(q):
        zx_hi[q], zx_lo[q] = split(zx[q])
        yd[OWN] += product(dd[q], near_z(q), NN)

    arrive("z3")
    finish_y(3)
    send("yx3")
    arrive("z4")
    finish_y(4)
    send("yx4")
    def offer(q):
        pd[q] = product(own_z(q), yd[q], TN)

    relay("z0", CUT_Z, "z1", "z2")
    finish_y(0)
    offer(0)
    arrive("zx3")
    gather_y(3)
    arrive("zx4")
    gather_y(4)
    relay("via1", CUT_V, "zx1")
    arrive(*all_of("z1", CUT_Z))
    finish_y(1)
    offer(1)
    send("p1")
    arrive(*all_of("z2", CUT_Z))
    finish_y(2)
    offer(2)
    send("p2")

    relay("via2", CUT_V, "zx2")
    arrive(*all_of("zx1", CUT_V))
    gather_y(1)
    arrive("p1", "p2")
    pd[0] += pr[0] + pr[1]
    send("s")

    @pl.loop(0, 5)
    def _(q):
        rd[q] = product(own_z(OWN), yd[q], TN)

    send("r1", "r2")
    arrive("zx0")
    gather_y(0)
    arrive(*all_of("zx2", CUT_V))
    gather_y(2)
    send(*all_of("y0", CUT), "y3", "y4")

    ad[OWN] = product(own_z(OWN), yd[OWN], TN)
    for q in (3, 4):
        arrive(f"yx{q}")
        ad[OWN] += product(near_z(q), yx[q - 3], TN)
        x = product(zr[q], yx[q - 3], TN) + product(own_z(q), yd[OWN], TN)
        an[q - 3] = keep(x, [n_has[q * 4 + k] for k in range(4)])
    arrive("s")
    ad[OWN] += sr[...]
    send(*all_of("a0", CUT), "a3", "a4")

    def finish_a(q):
        ad[q] = keep(rd[q] + product(near_z(q), yr[q], TN), own_flags(q))

    def finish_w(q):
        wd[q] = product(own_z(OWN), ad[q], NN)

    for q in (3, 4):
        arrive(f"y{q}")
        finish_a(q)
        finish_w(q)
    wd[OWN] = product(own_z(OWN), ad[OWN], NN) + (product(zd[3], an[0], NN) + product(zd[4], an[1], NN))
    arrive("r1", "r2")
    relay("y0", CUT, "y1", "y2")
    hop = [split(via[k]) for k in range(2)]
    y_near = split(yr[0])
    raw = [product(near_z(0), y_near, TN)] + [product(hop[k], y_near, TN) for k in range(2)]
    x0 = keep(rd[0] + raw[0], own_flags(0))
    x1, x2 = (keep(rr[k] + raw[k + 1], [n_has[k * 4 + i] for i in range(4)]) for k in range(2))
    qd[...] = product(near_z(0), x0, NN) + product(hop[0], x1, NN) + product(hop[1], x2, NN)
    send("u")
    ad[0] = x0
    fd[OWN] = jnp.zeros((WIDE, WIDE), jnp.float32)

    def start_f(*qs):
        raw = [product(own_z(q), ar[q], NN) for q in qs]
        ws = [split(keep(wd[q] + x, own_flags(q))) for q, x in zip(qs, raw)]
        for q, w in zip(qs, ws):
            fd[q] = product(w, zr[q], NT)
        own = [product(w, own_z(q), NT) for q, w in zip(qs, ws)]
        fd[OWN] += own[0] if len(qs) == 1 else own[0] + own[1]

    relay("a0", CUT, "a1", "a2")
    arrive("a3", "a4")
    start_f(3, 4)
    for q in (1, 2):
        arrive(*all_of(f"y{q}", CUT))
        finish_a(q)
    for q in (0, 1, 2):
        finish_w(q)
    start_f(0)

    def collect(dense, out):
        for r in range(2):
            for s in range(SLOTS):
                place = o_at[r * SLOTS + s]
                both = dense[lax.div(place, 2), r * BLK : (r + 1) * BLK]
                out[r * SLOTS + s] = jnp.where(lax.rem(place, 2) > 0, both[:, BLK:], both[:, :BLK])

    collect(ad, ox)
    arrive(*all_of("a1", CUT), *all_of("a2", CUT))
    start_f(1, 2)
    arrive("u")
    w_hi[...], w_lo[...] = split(wd[OWN] + ur[...])

    @pl.loop(0, 5, unroll=5)
    def _(q):
        fd[q] += product((w_hi[...], w_lo[...]), near_z(q), NT)

    fd[OWN] += product((w_hi[...], w_lo[...]), own_z(OWN), NT)
    collect(fd, of)
    for one in c.values():
        one.wait_send()


def deliver(x, f, out_x, out_f, sem):
    copies = [pltpu.make_async_copy(x, out_x, sem.at[0]), pltpu.make_async_copy(f, out_f, sem.at[1])]
    for one in copies:
        one.start()
    for one in copies:
        one.wait()


def shards(z_factor, z_columns, p_columns, d_density):
    tiles = (2 * SLOTS, BLK, BLK)
    wide = (WIDE, WIDE)
    f32 = jnp.float32
    counts = [6, 6, 5, 5, 6, 5, 2, 6, 5, 2, 6, 6, 3, 2, 0, 5, 2, 2, 0, 0]
    out_x, out_f = pl.pallas_call(
        kernel,
        out_shape=[pltpu.VMEM(tiles, f32)] * 2,
        in_specs=[pl.BlockSpec(memory_space=pltpu.HBM)] * 4,
        out_specs=[pl.BlockSpec(memory_space=pltpu.VMEM)] * 2,
        scratch_shapes=[pltpu.VMEM(tiles, f32)] * 2
        + [pltpu.VMEM((n,) + wide if n else wide, f32) for n in counts]
        + [pltpu.VMEM((n,) + wide if n else wide, jnp.bfloat16) for n in (6, 6, 5, 5, 0, 0)]
        + [pltpu.SMEM((SLOTS, ROWS), jnp.int32)] * 2
        + [pltpu.SMEM((n,), jnp.int32) for n in (24, 24, 24, 24, 16, 20)]
        + [pltpu.SemaphoreType.DMA((6,)), pltpu.SemaphoreType.DMA((48,)), pltpu.SemaphoreType.DMA((48,))],
        compiler_params=pltpu.CompilerParams(collective_id=0, has_side_effects=True, vmem_limit_bytes=48 * 1024 * 1024),
    )(*(pltpu.with_memory_space_constraint(x, pltpu.HBM) for x in (z_columns.T, p_columns.T, z_factor.reshape(tiles), d_density.reshape(tiles))))
    out_x, out_f = pl.pallas_call(
        deliver,
        out_shape=[pltpu.HBM(tiles, f32)] * 2,
        in_specs=[pl.BlockSpec(memory_space=pltpu.VMEM)] * 2,
        out_specs=[pl.BlockSpec(memory_space=pltpu.HBM)] * 2,
        scratch_shapes=[pltpu.SemaphoreType.DMA((2,))],
    )(*(pltpu.with_memory_space_constraint(x, pltpu.VMEM) for x in (out_x, out_f)))
    shape = z_factor.shape
    return out_x.reshape(shape), out_f.reshape(shape)


def solution(mesh):
    spec = P(("gx", "gy", "gz"), None, None, None)
    return jax.shard_map(shards, mesh=mesh, in_specs=(spec, P(), P(), spec), out_specs=(spec, spec), check_vma=False)
```
